32 devices in a mesh: grp: 2 (over x), exp: 8 (over z, y), tp: 2 (over core).
Axes of the slice: x: 2, y: 2, z: 4, core: 2. Of those that a mesh axis runs over, the one named last changes fastest.
Arguments:
- tokens: bfloat16 [4096, 2304], P(('grp', 'exp', 'tp')), parts along dimension 0, may hold values from -12 to 12
- router: bfloat16 [2304, 8], replicated, may hold values from -0.03125 to 0.03125
- expert_ids: int32 [4096, 4], P(('grp', 'exp', 'tp')), parts along dimension 0, may hold values from 0 to 7, all different within a row; in each aligned block of 128 rows (0 to 127, 128 to 255, ...) at most 80 rows name the same one
- gate_weight: bfloat16 [8, 2304, 1536], P('exp', None, 'tp'), may hold values from -0.125 to 0.125
- up_weight: bfloat16 [8, 2304, 1536], P('exp', None, 'tp'), may hold values from -0.125 to 0.125
- down_weight: bfloat16 [8, 1536, 2304], P('exp', 'tp'), may hold values from -0.15625 to 0.15625
Outputs:
- combined: bfloat16 [4096, 2304], P(('grp', 'exp', 'tp')), parts along dimension 0
The draws below stay inside these ranges and needn't reach their ends.
There are 2 independent parts, one for each index of `grp`. The reference program is written for one: setup_inputs(seed, part) draws one part's arguments, and reference() takes and returns one part's arrays. A program takes and returns all parts, laid end to end along the dimension named above; an argument that names none is the same for every part. Nothing has to cross between parts.
Inputs may be any that keep to these rules, and one draw needn't show every extreme that they name: `expert_ids`: each row names 4 different experts; among the 128 rows of one device no expert is named more than 80 times, a bound that some block reaches.
All inputs are finite; a program needn't handle non-finite values.
Results may differ from the reference program's by a relative error of at most 0.0068.
Values may be sent and summed in bfloat16 or wider, within the bound.
A program may use at most 128 MiB of HBM per device.

```python
import math
import jax
import jax.numpy as jnp
import numpy as np
from jax import lax

D = 2304
FF = 1536
TOP = 4
TOK_DEV = 128
EXPERTS = 8
CAP = 80
TOKENS = 2048
N_EXP = 8
N_TP = 2


def steps_of(own_key, extent, split, smallest, top_value):
    gain = 1.0
    for axis_at, shards_of in split:
        steps = jax.random.uniform(jax.random.fold_in(jax.random.fold_in(own_key, 6), axis_at), (shards_of,), jnp.float32, smallest / len(split), top_value / len(split))
        gain = gain * jnp.repeat(jnp.exp(steps), extent[axis_at] // shards_of).reshape((-1,) + (1,) * (len(extent) - 1 - axis_at))
    return gain


def assign_block(own_key, own, number, rows, amount, top, limit, slope):
    ranking = jax.random.permutation(own_key, amount)
    heavy_load, usual = shares(amount, rows * top, limit, slope, True), shares(amount, rows * top, limit, slope, False)
    places = jnp.arange(amount)

    def named(lengths, offset_by):
        used = int((lengths > 0).sum())
        fixed = max(1, used // 4)
        passed = fixed + (places - fixed + offset_by * (used - fixed)) % max(1, amount - fixed)
        return jnp.zeros((amount,), jnp.int32).at[ranking[jnp.where(places < fixed, places, passed)]].set(jnp.asarray(lengths, jnp.int32))

    lengths = jnp.where(number % 4 == 0, named(heavy_load, number // 4), named(usual, number - number // 4 - 1))
    mixed = jax.random.permutation(jax.random.fold_in(own, 3), amount)
    source_of, receiver = mixed[0:amount // 2 * 2:2], mixed[1:amount // 2 * 2:2]
    slack = jnp.minimum(lengths[source_of] - 1, limit - lengths[receiver]) // 2
    slack = jnp.where((source_of == ranking[0]) | (receiver == ranking[0]) | (lengths[receiver] == 0), 0, jnp.maximum(slack, 0))
    passed = jax.random.randint(jax.random.fold_in(own, 4), (amount // 2,), 0, 1 << 20) % (slack + 1)
    lengths = lengths.at[source_of].add(-passed).at[receiver].add(passed)
    members = jnp.searchsorted(jnp.cumsum(lengths), jnp.arange(rows * top), side="right").astype(jnp.int32)
    table = members.reshape(top, rows).T
    table = table[jax.random.permutation(jax.random.fold_in(own, 1), rows)]
    offset_by = jax.random.randint(jax.random.fold_in(own, 2), (rows, 1), 0, top)
    return jnp.take_along_axis(table, (jnp.arange(top)[None, :] + offset_by) % top, axis=1)


def shares(number_of, total, bound, slope, full):
    weights = [(1 << 20) // math.isqrt(rank ** slope) + 1 for rank in range(1, number_of + 1)]
    largest = bound if full else min(bound, max(-(-total // number_of), total * weights[0] // sum(weights)))
    least = 1 if total - largest >= number_of - 1 else 0
    counts, spare = [largest] + [least] * (number_of - 1), total - largest - least * (number_of - 1)
    while spare > 0:
        free = [i for i in range(1, number_of) if counts[i] < largest] or [i for i in range(1, number_of) if counts[i] < bound]
        pool, remaining = sum([weights[i] for i in free]), spare
        for i in free:
            extra = min(bound - counts[i], max(1, remaining * weights[i] // pool), spare)
            counts[i] = counts[i] + extra
            spare = spare - extra
    return np.array(counts)


def bell_draw(own_key, extent, width, limit, shards=(), kind=jnp.bfloat16):
    result = jax.random.normal(own_key, extent, jnp.float32) * width
    if len(shards) > 0:
        result = steps_of(own_key, extent, shards, -0.22, 0.18) * result
    return jnp.clip(result, min=-limit, max=limit).astype(kind)


def setup_inputs(seed: int = 0, part: int = 0) -> dict:
    streams_of = jax.random.split(jax.random.key(seed), 7)
    own_keys = jax.random.split(jax.random.fold_in(streams_of[6], part), 7)
    tokens = bell_draw(own_keys[0], (TOKENS, D), 2.5, 12.0, ((0, 16),))
    router = bell_draw(streams_of[1], (D, EXPERTS), (16 * D) ** -0.5, 0.03125)
    expert_ids_keys = jax.random.split(jax.random.fold_in(own_keys[2], 1), TOKENS // TOK_DEV)
    expert_ids_turns = jax.random.permutation(jax.random.fold_in(own_keys[2], 3), TOKENS // TOK_DEV)
    expert_ids = jax.vmap(lambda own, number: assign_block(jax.random.fold_in(own_keys[2], 2), own, number, TOK_DEV, EXPERTS, TOP, CAP, 1))(expert_ids_keys, expert_ids_turns).reshape((TOKENS, TOP))
    gate_weight = bell_draw(streams_of[3], (EXPERTS, D, FF), D ** -0.5, 0.125, ((0, 8), (2, 2)))
    up_weight = bell_draw(streams_of[4], (EXPERTS, D, FF), D ** -0.5, 0.125, ((0, 8), (2, 2)))
    down_weight = bell_draw(streams_of[5], (EXPERTS, FF, D), FF ** -0.5, 0.15625, ((0, 8), (1, 2)))
    return {"tokens": tokens, "router": router, "expert_ids": expert_ids, "gate_weight": gate_weight, "up_weight": up_weight, "down_weight": down_weight}


def slot_numbers(choices_flat, expert_count):
    onehot = (choices_flat[:, None] == jnp.arange(expert_count, dtype=jnp.int32)[None, :]).astype(jnp.int32)
    before = jnp.cumsum(onehot, axis=0) - onehot
    return jnp.sum(before * onehot, axis=1).astype(jnp.int32)


def router_gates(tokens, router, expert_ids):
    logits = jnp.dot(tokens, router, preferred_element_type=jnp.float32)
    chosen = jnp.take_along_axis(logits, expert_ids, axis=1)
    raised = jnp.exp(chosen)
    return raised / jnp.sum(raised, axis=1, keepdims=True)


def swiglu_part(slot_rows, gate_part, up_part, down_part):
    gate_act = jnp.dot(slot_rows, gate_part, preferred_element_type=jnp.float32)
    lifted = jnp.dot(slot_rows, up_part, preferred_element_type=jnp.float32)
    gate_act = jnp.minimum(gate_act, 7.0)
    lifted = jnp.clip(lifted, -7.0, 7.0)
    hidden = ((lifted + 1.0) * gate_act * jax.nn.sigmoid(1.702 * gate_act)).astype(jnp.bfloat16)
    return jnp.dot(hidden, down_part, preferred_element_type=jnp.float32).astype(jnp.bfloat16)


def reference(tokens, router, expert_ids, gate_weight, up_weight, down_weight):
    blocks = N_EXP * N_TP
    gate_share = router_gates(tokens, router, expert_ids)
    flat_ids = expert_ids.reshape(blocks, TOK_DEV * TOP)
    slot_index = jax.vmap(lambda id_row: slot_numbers(id_row, EXPERTS))(flat_ids)
    block_of = jnp.arange(blocks, dtype=jnp.int32)[:, None]
    token_of = block_of * TOK_DEV + jnp.arange(TOK_DEV * TOP, dtype=jnp.int32)[None, :] // TOP
    column = (block_of * CAP + slot_index).reshape(-1)
    expert_flat = flat_ids.reshape(-1)
    token_table = jnp.zeros((EXPERTS, blocks * CAP), jnp.int32).at[expert_flat, column].set(token_of.reshape(-1))
    weight_table = jnp.zeros((EXPERTS, blocks * CAP), jnp.float32).at[expert_flat, column].set(gate_share.reshape(-1))
    share_width = FF // N_TP

    def one_expert(running, expert):
        slot_rows = tokens[token_table[expert]]
        summed = jnp.zeros((blocks * CAP, D), jnp.float32)
        for part_index in range(N_TP):
            start_col = part_index * share_width
            partial_value = swiglu_part(slot_rows, gate_weight[expert][:, start_col:start_col + share_width], up_weight[expert][:, start_col:start_col + share_width], down_weight[expert][start_col:start_col + share_width, :])
            summed = summed + lax.optimization_barrier(partial_value).astype(jnp.float32)
        output = lax.optimization_barrier(summed.astype(jnp.bfloat16)).astype(jnp.float32)
        return running.at[token_table[expert]].add(weight_table[expert][:, None] * output), None

    running = lax.scan(one_expert, jnp.zeros((TOKENS, D), jnp.float32), jnp.arange(EXPERTS, dtype=jnp.int32))[0]
    return running.astype(jnp.bfloat16)
```

```python
import functools

import jax
import jax.numpy as jnp
from jax import lax
from jax.experimental import pallas as pl
from jax.experimental.pallas import tpu as pltpu
from jax.sharding import PartitionSpec as P

MESH = pl.DeviceIdType.MESH
STEPS = 4
F32 = jnp.float32
BF16 = jnp.bfloat16


def moe_kernel(
    cap,
    chunks,
    tok_ref,
    router_ref,
    ids_ref,
    wg_hbm,
    wu_hbm,
    wd_hbm,
    out_ref,
    wg,
    wu,
    wd,
    tok,
    gates,
    slots,
    ypack,
    own,
    tpout,
    tpin,
    yret,
    comb,
    acc,
    rout,
    inbox,
    w_sem,
    tok_s,
    tok_r,
    gate_s,
    gate_r,
    ys_s,
    ys_r,
    t0_s,
    t0_r,
    t2_s,
    t2_r,
    tp_s,
    tp_r,
    yr_s,
    yr_r,
    rs_s,
    rs_r,
):
    rows, width = tok_ref.shape
    experts = router_ref.shape[1]
    top = ids_ref.shape[1]
    grp, exp, tp = lax.axis_index("grp"), lax.axis_index("exp"), lax.axis_index("tp")
    z, y = exp // 2, exp % 2
    adj_z = z + 1 - 2 * (z % 2)
    across_z = 3 - z
    other_exp = exp + 1 - 2 * y
    adj = (grp, adj_z * 2 + y, tp)
    across = (grp, across_z * 2 + y, tp)
    ynb = (grp, other_exp, tp)
    tpn = (grp, exp, 1 - tp)
    middle = jnp.logical_or(z == 1, z == 2)
    edge = jnp.logical_or(z == 0, z == 3)

    loads = [
        pltpu.make_async_copy(src.at[0], dst, w_sem.at[n])
        for n, (src, dst) in enumerate(((wg_hbm, wg), (wu_hbm, wu), (wd_hbm, wd)))
    ]
    for load in loads:
        load.start()

    barrier = pltpu.get_barrier_semaphore()
    for peer in (adj, ynb, tpn):
        pl.semaphore_signal(barrier, inc=1, device_id=peer, device_id_type=MESH)

    @pl.when(middle)
    def _():
        pl.semaphore_signal(barrier, inc=1, device_id=across, device_id_type=MESH)
        pl.semaphore_wait(barrier, 4)

    @pl.when(edge)
    def _():
        pl.semaphore_wait(barrier, 3)

    def remote(src, dst, send, recv, peer):
        return pltpu.make_async_remote_copy(
            src_ref=src,
            dst_ref=dst,
            send_sem=send,
            recv_sem=recv,
            device_id=peer,
            device_id_type=MESH,
        )

    def tok_copy(n, source, target, peer):
        src = tok_ref if source == 0 else tok.at[source - 1]
        return remote(src, tok.at[target - 1], tok_s.at[n], tok_r.at[target - 1], peer)

    def gate_copy(n, source, target, peer):
        return remote(gates.at[source], gates.at[target], gate_s.at[n], gate_r.at[target - 1], peer)

    hops = ((0, 0, 1, adj), (1, 0, 2, across), (2, 1, 3, across), (3, 2, 2, adj), (4, 3, 3, adj))

    tok_copy(*hops[0]).start()

    @pl.when(middle)
    def _():
        tok_copy(*hops[1]).start()

    logits = jnp.dot(tok_ref[...], router_ref[...], preferred_element_type=F32)
    lane = lax.broadcasted_iota(jnp.int32, (rows, experts), 1)
    ids = ids_ref[...]
    chosen = jnp.zeros((rows, experts), F32)
    for k in range(top):
        chosen = jnp.where(lane == ids[:, k : k + 1], 1.0, chosen)
    raised = jnp.where(chosen > 0.0, jnp.exp(logits), 0.0)
    share = raised / jnp.sum(raised, axis=1, keepdims=True)
    wide = jnp.concatenate([share, jnp.zeros((rows, 128 - experts), F32)], axis=1)
    gates[0] = wide.T[:experts]
    gate_copy(*hops[0]).start()

    @pl.when(middle)
    def _():
        gate_copy(*hops[1]).start()

    def placing(i, weighted):
        g8 = gates[i]
        m8 = jnp.where(g8 > 0.0, 1.0, 0.0)
        before = lax.broadcasted_iota(jnp.int32, (rows, rows), 0)
        after = lax.broadcasted_iota(jnp.int32, (rows, rows), 1)
        earlier = jnp.where(before < after, 1.0, 0.0).astype(BF16)
        pos8 = jnp.dot(m8.astype(BF16), earlier, preferred_element_type=F32)
        pos8 = jnp.where(m8 > 0.0, pos8, -1000.0)
        which = lax.broadcasted_iota(jnp.int32, (experts, rows), 0)

        def pick(table, number):
            return jnp.sum(jnp.where(which == number, table, 0.0), axis=0, keepdims=True)

        slot = lax.broadcasted_iota(jnp.int32, (2 * cap, rows), 0)
        mine = slot < cap
        wanted = jnp.where(mine, pick(pos8, exp), pick(pos8, other_exp) + float(cap))
        value = jnp.where(mine, pick(g8, exp), pick(g8, other_exp)) if weighted else 1.0
        return jnp.where(wanted == slot.astype(F32), value, 0.0)

    def ysend(i):
        return remote(ypack.at[i], slots.at[i, pl.ds(cap, cap)], ys_s.at[i], ys_r.at[i], ynb)

    def tsend0(i):
        return remote(
            slots.at[i, pl.ds(0, cap)], slots.at[i, pl.ds(2 * cap, cap)], t0_s.at[i], t0_r.at[i], tpn
        )

    def tsend2(i):
        return remote(
            slots.at[i, pl.ds(cap, cap)], slots.at[i, pl.ds(3 * cap, cap)], t2_s.at[i], t2_r.at[i], tpn
        )

    def psend(i):
        return remote(tpout.at[i], tpin.at[i], tp_s.at[i], tp_r.at[i], tpn)

    def yback(i):
        return remote(yret.at[i], comb.at[i, pl.ds(cap, cap)], yr_s.at[i], yr_r.at[i], ynb)

    def step_pack(i):
        place = placing(i, False).astype(BF16)
        block = tok_ref if i == 0 else tok.at[i - 1]
        ypack[i] = jnp.dot(place[cap:], block[...], preferred_element_type=F32).astype(BF16)
        ysend(i).start()
        slots[i, pl.ds(0, cap)] = jnp.dot(
            place[:cap], block[...], preferred_element_type=F32
        ).astype(BF16)
        tsend0(i).start()

    def step_share(i):
        ysend(i).wait_recv()
        tsend2(i).start()

    def step_experts(i):
        tsend0(i).wait_recv()
        tsend2(i).wait_recv()
        block = slots[i]
        gate_act = jnp.minimum(jnp.dot(block, wg[...], preferred_element_type=F32), 7.0)
        lifted = jnp.clip(jnp.dot(block, wu[...], preferred_element_type=F32), -7.0, 7.0)
        hidden = ((lifted + 1.0) * gate_act * jax.nn.sigmoid(1.702 * gate_act)).astype(BF16)
        part = width // 3
        for c in range(3):
            at = pl.ds(c * part, part)
            result = jnp.dot(hidden, wd[:, at], preferred_element_type=F32)
            own[:, at] = result[: 2 * cap]
            tpout[i, :, at] = result[2 * cap :].astype(BF16)
        psend(i).start()

    def step_join(i):
        psend(i).wait_recv()
        yret[i] = (own[cap:] + tpin[i, pl.ds(cap, cap)].astype(F32)).astype(BF16)
        yback(i).start()
        comb[i, pl.ds(0, cap)] = (own[:cap] + tpin[i, pl.ds(0, cap)].astype(F32)).astype(BF16)

    def step_combine(i):
        yback(i).wait_recv()
        weight = placing(i, True)
        high = weight.astype(BF16)
        low = (weight - high.astype(F32)).astype(BF16)
        block = comb[i]
        turned = (((0,), (0,)), ((), ()))
        acc[i] = lax.dot_general(high, block, turned, preferred_element_type=F32) + lax.dot_general(
            low, block, turned, preferred_element_type=F32
        )

    def arrive(phase):
        def take(step):
            tok_copy(0, 0, step, adj).wait_recv()
            gate_copy(0, 0, step, adj).wait_recv()

        def give(n):
            tok_copy(*hops[n]).start()
            gate_copy(*hops[n]).start()

        @pl.when(edge)
        def _():
            take(phase)

        @pl.when(middle)
        def _():
            if phase == 1:
                take(1)
                give(2)
                take(2)
                give(3)
            elif phase == 2:
                take(3)
                give(4)

    span = width // chunks

    def sum_copy(i, slot, c, peer):
        at = pl.ds(c * span, span)
        return remote(
            rout.at[i - 1, :, at],
            inbox.at[slot, :, at],
            rs_s.at[(i - 1) * chunks + c],
            rs_r.at[slot * chunks + c],
            peer,
        )

    def edge_send(i):
        @pl.when(edge)
        def _():
            for c in range(chunks):
                at = pl.ds(c * span, span)
                rout[i - 1, :, at] = acc[i, :, at].astype(BF16)
                sum_copy(i, i - 1, c, adj).start()

    def middle_send(i, arrived, slot, peer):
        for c in range(chunks):
            at = pl.ds(c * span, span)
            sum_copy(1, arrived, c, adj).wait_recv()
            rout[i - 1, :, at] = (acc[i, :, at] + inbox[arrived, :, at].astype(F32)).astype(BF16)
            sum_copy(i, slot, c, peer).start()

    step_pack(0)
    step_share(0)
    arrive(1)
    step_pack(1)
    for load in loads:
        load.wait()
    step_experts(0)
    step_join(0)
    step_share(1)
    arrive(2)
    step_pack(2)
    step_combine(0)
    step_experts(1)
    step_join(1)
    step_share(2)
    arrive(3)
    step_pack(3)
    step_combine(1)
    edge_send(1)
    step_experts(2)
    step_join(2)
    step_share(3)
    step_experts(3)
    step_join(3)
    step_combine(2)
    edge_send(2)
    step_combine(3)
    edge_send(3)

    @pl.when(middle)
    def _():
        middle_send(2, 1, 3, across)
        middle_send(3, 2, 4, across)
        middle_send(1, 4, 0, adj)
        for c in range(chunks):
            at = pl.ds(c * span, span)
            sum_copy(1, 0, c, adj).wait_recv()
            sum_copy(1, 3, c, adj).wait_recv()
            out_ref[:, at] = (
                acc[0, :, at] + inbox[0, :, at].astype(F32) + inbox[3, :, at].astype(F32)
            ).astype(BF16)

    @pl.when(edge)
    def _():
        for c in range(chunks):
            at = pl.ds(c * span, span)
            sum_copy(1, 0, c, adj).wait_recv()
            out_ref[:, at] = (acc[0, :, at] + inbox[0, :, at].astype(F32)).astype(BF16)

    tok_copy(*hops[0]).wait_send()
    gate_copy(*hops[0]).wait_send()

    @pl.when(middle)
    def _():
        for n in range(1, 5):
            tok_copy(*hops[n]).wait_send()
            gate_copy(*hops[n]).wait_send()

    for i in range(STEPS):
        for copy in (ysend(i), tsend0(i), tsend2(i), psend(i), yback(i)):
            copy.wait_send()
    for i in range(1, STEPS):
        for c in range(chunks):
            sum_copy(i, 0, c, adj).wait_send()


def on_line(tokens, router, expert_ids, gate_weight, up_weight, down_weight):
    rows, width = tokens.shape
    top = expert_ids.shape[1]
    experts = router.shape[1]
    hidden = gate_weight.shape[2]
    cap = capacity_of(rows, top, experts)
    chunks = 2
    dma = pltpu.SemaphoreType.DMA
    vmem = pl.BlockSpec(memory_space=pltpu.VMEM)
    hbm = pl.BlockSpec(memory_space=pl.ANY)
    flops = 6 * STEPS * 4 * cap * width * hidden
    return pl.pallas_call(
        functools.partial(moe_kernel, cap, chunks),
        out_shape=jax.ShapeDtypeStruct((rows, width), BF16),
        in_specs=[vmem, vmem, vmem, hbm, hbm, hbm],
        out_specs=vmem,
        scratch_shapes=[
            pltpu.VMEM((width, hidden), BF16),
            pltpu.VMEM((width, hidden), BF16),
            pltpu.VMEM((hidden, width), BF16),
            pltpu.VMEM((STEPS - 1, rows, width), BF16),
            pltpu.VMEM((STEPS, experts, rows), F32),
            pltpu.VMEM((STEPS, 4 * cap, width), BF16),
            pltpu.VMEM((STEPS, cap, width), BF16),
            pltpu.VMEM((2 * cap, width), F32),
            pltpu.VMEM((STEPS, 2 * cap, width), BF16),
            pltpu.VMEM((STEPS, 2 * cap, width), BF16),
            pltpu.VMEM((STEPS, cap, width), BF16),
            pltpu.VMEM((STEPS, 2 * cap, width), BF16),
            pltpu.VMEM((STEPS, rows, width), F32),
            pltpu.VMEM((STEPS - 1, rows, width), BF16),
            pltpu.VMEM((5, rows, width), BF16),
            dma((3,)),
            dma((5,)),
            dma((3,)),
            dma((5,)),
            dma((3,)),
        ]
        + [dma((STEPS,))] * 10
        + [dma((3 * chunks,)), dma((5 * chunks,))],
        compiler_params=pltpu.CompilerParams(
            collective_id=0, has_side_effects=True, vmem_limit_bytes=56 * 2**20
        ),
        cost_estimate=pl.CostEstimate(
            flops=flops, bytes_accessed=6 * width * hidden, transcendentals=0
        ),
    )(tokens, router, expert_ids, gate_weight, up_weight, down_weight)


def capacity_of(rows, top, experts):
    return min(rows, max(2, (5 * rows * top + 4 * experts - 1) // (4 * experts)))


def slot_numbers(choices_flat, expert_count):
    onehot = (choices_flat[:, None] == jnp.arange(expert_count, dtype=jnp.int32)[None, :]).astype(
        jnp.int32
    )
    before = jnp.cumsum(onehot, axis=0) - onehot
    return jnp.sum(before * onehot, axis=1)


def router_gates(tokens, router, expert_ids):
    logits = jnp.dot(tokens, router, preferred_element_type=jnp.float32)
    chosen = jnp.take_along_axis(logits, expert_ids, axis=1)
    raised = jnp.exp(chosen)
    return raised / jnp.sum(raised, axis=1, keepdims=True)


def swiglu_part(slot_rows, gate_part, up_part, down_part):
    gate_act = jnp.dot(slot_rows, gate_part, preferred_element_type=jnp.float32)
    lifted = jnp.dot(slot_rows, up_part, preferred_element_type=jnp.float32)
    gate_act = jnp.minimum(gate_act, 7.0)
    lifted = jnp.clip(lifted, -7.0, 7.0)
    hidden = ((lifted + 1.0) * gate_act * jax.nn.sigmoid(1.702 * gate_act)).astype(jnp.bfloat16)
    return jnp.dot(hidden, down_part, preferred_element_type=jnp.float32).astype(jnp.bfloat16)


def on_device(tokens, router, expert_ids, gate_weight, up_weight, down_weight):
    tok_rows, model_width = tokens.shape
    top_count = expert_ids.shape[1]
    experts_all = router.shape[1]
    capacity = capacity_of(tok_rows, top_count, experts_all)
    gate_share = router_gates(tokens, router, expert_ids)
    flat_ids = expert_ids.reshape(-1)
    target = flat_ids * capacity + slot_numbers(flat_ids, experts_all)
    slot_ids = jnp.arange(experts_all * capacity, dtype=jnp.int32)
    placing = (slot_ids[:, None] == target[None, :]).astype(jnp.bfloat16)
    placing = placing.reshape(experts_all * capacity, tok_rows, top_count).sum(axis=2)
    outgoing = jnp.dot(placing, tokens, preferred_element_type=jnp.float32).astype(jnp.bfloat16)
    outgoing = outgoing.reshape(experts_all, capacity, model_width)
    gate_local = gate_weight[0]
    up_local = up_weight[0]
    down_local = down_weight[0]
    tp_count = lax.axis_size("tp")
    received = lax.all_to_all(outgoing, "exp", split_axis=0, concat_axis=0, tiled=True)
    gathered = lax.all_gather(received, "tp", axis=0, tiled=True)
    sources = gathered.shape[0]
    slot_count = gathered.shape[1]
    flattened = gathered.reshape(sources * slot_count, model_width)
    partial_value = swiglu_part(flattened, gate_local, up_local, down_local).reshape(
        sources, slot_count, model_width
    )
    swapped = lax.all_to_all(partial_value, "tp", split_axis=0, concat_axis=0, tiled=True)
    own_count = received.shape[0]
    slot_count = received.shape[1]
    paired = swapped.reshape(tp_count, own_count, slot_count, model_width).astype(jnp.float32)
    own_share = jnp.sum(paired, axis=0).astype(jnp.bfloat16)
    results = lax.all_to_all(own_share, "exp", split_axis=0, concat_axis=0, tiled=True)
    flat_results = results.reshape(experts_all * capacity, model_width)
    picked = flat_results[target].reshape(tok_rows, top_count, model_width).astype(jnp.float32)
    combined = jnp.sum(gate_share[:, :, None] * picked, axis=1)
    return combined.astype(jnp.bfloat16)


def solution(mesh):
    placed = (
        P(("grp", "exp", "tp"), None),
        P(),
        P(("grp", "exp", "tp"), None),
        P("exp", None, "tp"),
        P("exp", None, "tp"),
        P("exp", "tp", None),
    )
    lined = mesh.shape["exp"] == 8 and mesh.shape["tp"] == 2
    return jax.shard_map(
        on_line if lined else on_device,
        mesh=mesh,
        in_specs=placed,
        out_specs=P(("grp", "exp", "tp"), None),
        check_vma=False,
    )
```
